32 devices in a mesh: frame: 16 (over z, x, core), tile: 2 (over y).
Axes of the slice: x: 2, y: 2, z: 4, core: 2. Of those that a mesh axis runs over, the one named last changes fastest.
Arguments:
- queries: bfloat16 [16, 2, 64, 5120], P('frame', 'tile'), may hold values from -6 to 6
- keys: bfloat16 [16, 2, 64, 5120], P('frame', 'tile'), may hold values from -6 to 6
- values: bfloat16 [16, 2, 64, 5120], P('frame', 'tile'), may hold values from -6 to 6
- step_index: int32 [16], P('frame'), may hold values from 0 to 3
- frame_index: int32 [16], P('frame'), may hold values from 0 to 9
- window_mask: int32 [40, 9], replicated, may hold values 0 or 1
- history_mask: int32 [16, 5], P('frame'), may hold values 0 or 1
- step_gain: float32 [4, 40], replicated, may hold values from 0.5 to 2
Outputs:
- output: bfloat16 [16, 2, 64, 5120], P('frame', 'tile')
The draws below stay inside these ranges and needn't reach their ends.
All inputs are finite; a program needn't handle non-finite values. No bound on the sum of `history_mask` on one device may be relied on, other than what follows from the above.
Results may differ from the reference program's by a relative error of at most 0.0095.
Values may be sent and summed in bfloat16 or wider, within the bound.
No kernel may reach another device: no remote copies, remote signals or barrier semaphores. Data moves between devices by JAX's collectives and lax.ppermute only.
A program may use at most 128 MiB of HBM per device.

```python
import math
import jax
import jax.numpy as jnp
from jax import lax

HEADS = 40
HD = 128
TH = 8
TW = 8
BLK = 4
WIN = 5
STEPS = 4
FRAMES = 16
TILES = 2
FRAME_TOK = 128
C = 5120


def shared_draw(key):
    shape = (FRAMES, TILES, TH * TW, C)
    query_base = jax.random.truncated_normal(jax.random.fold_in(key, 11), -6.0, 6.0, shape, jnp.float32)
    key_base = jax.random.truncated_normal(jax.random.fold_in(key, 12), -6.0, 6.0, shape, jnp.float32)
    return (query_base, key_base)


def draw_queries(key, part):
    return shared_draw(key)[0].astype(jnp.bfloat16)


def draw_keys(key, part):
    return shared_draw(key)[1].astype(jnp.bfloat16)


def plant(drawn, stream_key, low, top_value):
    place = [jax.random.randint(jax.random.fold_in(stream_key, axis), (), 0, length) for axis, length in enumerate(drawn.shape)]
    main_axis = drawn.shape.index(max(drawn.shape))
    next_to = place[:main_axis] + [(place[main_axis] + 1) % drawn.shape[main_axis]] + place[main_axis + 1:]
    return drawn.at[tuple(place)].set(low).at[tuple(next_to)].set(top_value)


def shard_levels(stream_key, shape, shards, smallest, top_value):
    gain = 1.0
    for dim, blocks in shards:
        steps = jax.random.uniform(jax.random.fold_in(jax.random.fold_in(stream_key, 6), dim), (blocks,), jnp.float32, smallest / len(shards), top_value / len(shards))
        gain = gain * jnp.repeat(jnp.exp(steps), shape[dim] // blocks).reshape((-1,) + (1,) * (len(shape) - 1 - dim))
    return gain


def scatter_about(key, extent, width, most, split=(), kind=jnp.bfloat16):
    values = jax.random.normal(key, extent, jnp.float32) * width
    if len(split) > 0:
        values = shard_levels(key, extent, split, -0.22, 0.18) * values
    return jnp.clip(values, min=-most, max=most).astype(kind)


def setup_inputs(seed: int = 0) -> dict:
    arg_keys = jax.random.split(jax.random.key(seed), 9)
    queries = draw_queries(jax.random.fold_in(arg_keys[8], 71), 0)
    keys = draw_keys(jax.random.fold_in(arg_keys[8], 71), 0)
    values = scatter_about(arg_keys[2], (FRAMES, TILES, TH * TW, C), 1.0, 6.0, ((0, 16), (1, 2)))
    step_index = plant(jax.random.randint(arg_keys[3], (FRAMES,), 0, STEPS), jax.random.fold_in(arg_keys[3], 1), 0, STEPS - 1).astype(jnp.int32)
    frame_index = plant(jax.random.randint(arg_keys[4], (FRAMES,), 0, 2 * WIN), jax.random.fold_in(arg_keys[4], 1), 0, (2 * WIN) - 1).astype(jnp.int32)
    window_mask = plant((jax.random.randint(arg_keys[5], (HEADS, 9), 0, 2) < 1).astype(jnp.int32), jax.random.fold_in(arg_keys[5], 1), 0, 1)
    history_mask = plant((jax.random.randint(arg_keys[6], (FRAMES, WIN), 0, 4) < 3).astype(jnp.int32), jax.random.fold_in(arg_keys[6], 1), 0, 1)
    step_gain = jnp.clip(jnp.exp(jax.random.uniform(arg_keys[7], (STEPS, HEADS), jnp.float32, math.log(0.5), math.log(2.0))), 0.5, 2.0)
    return {"queries": queries, "keys": keys, "values": values, "step_index": step_index, "frame_index": frame_index, "window_mask": window_mask, "history_mask": history_mask, "step_gain": step_gain}


def token_place(positions, tile_cols):
    tile_of = positions // (TH * TW)
    within = positions % (TH * TW)
    grid_row = tile_of // tile_cols * TH + within // TW
    grid_col = tile_of % tile_cols * TW + within % TW
    return (grid_row, grid_col)

def offset_code(query_row, query_col, key_row, key_col):
    row_step = key_row // BLK - query_row // BLK
    across = key_col // BLK - query_col // BLK
    nearby = (jnp.abs(row_step) <= 1) & (jnp.abs(across) <= 1)
    return jnp.where(nearby, (row_step + 1) * 3 + across + 1, -1).astype(jnp.int32)

def window_allow(offset_ids, mask_rows):
    allowed = (offset_ids == 4)[None]
    for offset in range(9):
        allowed = allowed | (offset_ids == offset)[None] & (mask_rows[:, offset] == 1)[:, None, None]
    return allowed

def reference(queries, keys, values, step_index, frame_index, window_mask, history_mask, step_gain):
    tile_cols = min(TILES, 4)
    scale_factor = 1.0 / math.sqrt(HD)
    positions = jnp.arange(FRAME_TOK, dtype=jnp.int32)
    grid_row, grid_col = token_place(positions, tile_cols)
    offset_ids = offset_code(grid_row[:, None], grid_col[:, None], grid_row[None, :], grid_col[None, :])
    flat_q = queries.reshape(FRAMES, FRAME_TOK, HEADS, HD)
    flat_k = keys.reshape(FRAMES, FRAME_TOK, HEADS, HD)
    flat_v = values.reshape(FRAMES, FRAME_TOK, HEADS, HD)
    distance = jnp.arange(1, WIN + 1, dtype=jnp.int32)

    def one_group(group_id):
        source = group_id - distance
        usable = (history_mask[group_id] == 1) & (distance <= frame_index[group_id]) & (source >= 0)
        source = jnp.maximum(source, 0).astype(jnp.int32)
        past_k = flat_k[source]
        past_v = flat_v[source]
        head_gains = step_gain[step_index[group_id]]

        def one_head(head_id):
            query_h = flat_q[group_id, :, head_id].astype(jnp.float32)
            own_k = flat_k[group_id, :, head_id].astype(jnp.float32)
            allowed = window_allow(offset_ids, window_mask[head_id][None, :])[0]
            own_s = jnp.dot(query_h, own_k.T, precision=lax.Precision.HIGHEST) * scale_factor
            own_s = jnp.where(allowed, own_s, -jnp.inf)
            past_s = jnp.einsum('qd,wkd->qwk', query_h, past_k[:, :, head_id].astype(jnp.float32), precision=lax.Precision.HIGHEST) * scale_factor
            past_s = jnp.where(usable[None, :, None], past_s, -jnp.inf).reshape(FRAME_TOK, WIN * FRAME_TOK)
            scores = jnp.concatenate([own_s, past_s], axis=1)
            row_max = lax.optimization_barrier(jnp.max(scores, axis=1, keepdims=True))
            weights = jnp.exp(scores - row_max)
            denominator = lax.optimization_barrier(jnp.sum(weights, axis=1, keepdims=True))
            all_values = jnp.concatenate([flat_v[group_id, :, head_id][None], past_v[:, :, head_id]], axis=0)
            all_values = all_values.reshape((WIN + 1) * FRAME_TOK, HD)
            blended = jnp.dot(weights.astype(jnp.bfloat16), all_values, preferred_element_type=jnp.float32)
            return blended / denominator * head_gains[head_id]
        per_head = lax.map(one_head, jnp.arange(HEADS, dtype=jnp.int32))
        return jnp.transpose(per_head, (1, 0, 2)).reshape(FRAME_TOK, C).astype(jnp.bfloat16)
    result = lax.map(one_group, jnp.arange(FRAMES, dtype=jnp.int32))
    return result.reshape(FRAMES, TILES, TH * TW, C)
```

```python
import functools
import math

import jax
import jax.numpy as jnp
from jax import lax
from jax.experimental import pallas as pl
from jax.experimental.pallas import tpu as pltpu
from jax.sharding import PartitionSpec as P

HEADS = 40
HD = 128
TH = 8
TW = 8
BLK = 4
WIN = 5
STEPS = 4

NEG_BIG = -1e30
CHUNKS = (2, 3)


def group_frames(frame_count, tile_count):
    return max(
        g
        for g in range(1, frame_count + 1)
        if frame_count % g == 0 and HEADS % (g * tile_count) == 0
    )


def first_needed(hop, group):
    return max(0, hop * group - WIN)


def pack(arrays, members, head_share, start, count):
    tokens = arrays[0].shape[0]
    width = count * HD

    def body(*refs):
        out = refs[-1]
        for n in range(members):
            for a, ref in enumerate(refs[:-1]):
                out[n, a] = ref[:, pl.ds((n * head_share + start) * HD, width)]

    vmem = pl.BlockSpec(memory_space=pltpu.VMEM)
    return pl.pallas_call(
        body,
        out_shape=jax.ShapeDtypeStruct((members, len(arrays), tokens, width), jnp.bfloat16),
        in_specs=[vmem] * len(arrays),
        out_specs=vmem,
    )(*arrays)


def unpack(parts, starts, head_share):
    members, tokens = parts[0].shape[:2]

    def body(*refs):
        out = refs[-1]
        for start, ref in zip(starts, refs[:-1]):
            for n in range(members):
                out[:, pl.ds((n * head_share + start) * HD, ref.shape[-1])] = ref[n]

    vmem = pl.BlockSpec(memory_space=pltpu.VMEM)
    return pl.pallas_call(
        body,
        out_shape=jax.ShapeDtypeStruct((tokens, members * head_share * HD), jnp.bfloat16),
        in_specs=[vmem] * len(parts),
        out_specs=vmem,
    )(*parts)


def attend(query, own_kv, hop_kv, bias, past_bias, gains, group):
    members, _, tokens, width = query.shape
    tiles = members // group
    frame_tok = tiles * tokens
    heads = width // HD
    factor = math.log2(math.e) / math.sqrt(HD)
    hops = len(hop_kv)

    def body(*refs):
        past_ref, gain_ref, q_ref, own_ref = refs[:4]
        hop_refs = refs[4 : 4 + hops]
        bias_ref, out_ref = refs[4 + hops :]

        def frame_of(ref, frame, which, lanes):
            return ref[frame * tiles : (frame + 1) * tiles, which, :, lanes].reshape(frame_tok, HD)

        def source(rel):
            if rel >= 0:
                return own_ref, rel
            hop = -(rel // group)
            return hop_refs[hop - 1], rel + hop * group - first_needed(hop, group)

        def one_head(h):
            lanes = pl.ds(h * HD, HD)
            own_bias = bias_ref[h]
            for j in range(group):
                q = frame_of(q_ref, j, 0, lanes)
                scores = []
                for d in range(WIN + 1):
                    ref, frame = source(j - d)
                    k = frame_of(ref, frame, 0, lanes)
                    s = lax.dot_general(
                        q, k, (((1,), (1,)), ((), ())), preferred_element_type=jnp.float32
                    )
                    s = s * factor
                    scores.append(s + own_bias if d == 0 else s + past_ref[j, d - 1])
                top = scores[0]
                for s in scores[1:]:
                    top = jnp.maximum(top, s)
                top = jnp.max(top, axis=1, keepdims=True)
                total = None
                blended = None
                for d in range(WIN + 1):
                    ref, frame = source(j - d)
                    v = frame_of(ref, frame, 1, lanes)
                    p = jnp.exp2(scores[d] - top)
                    total = p if total is None else total + p
                    part = jnp.dot(p.astype(jnp.bfloat16), v, preferred_element_type=jnp.float32)
                    blended = part if blended is None else blended + part
                norm = jnp.sum(total, axis=1, keepdims=True)
                result = (blended * (gain_ref[j, h] / norm)).astype(jnp.bfloat16)
                out_ref[j * tiles : (j + 1) * tiles, :, lanes] = result.reshape(tiles, tokens, HD)

        for h in range(heads):
            one_head(h)

    smem = pl.BlockSpec(memory_space=pltpu.SMEM)
    vmem = pl.BlockSpec(memory_space=pltpu.VMEM)
    keys = frame_tok * (WIN + 1)
    return pl.pallas_call(
        body,
        out_shape=jax.ShapeDtypeStruct((members, tokens, width), jnp.bfloat16),
        in_specs=[smem, smem] + [vmem] * (3 + hops),
        out_specs=vmem,
        cost_estimate=pl.CostEstimate(
            flops=4 * group * heads * frame_tok * keys * HD,
            bytes_accessed=2 * width * tokens * members * 6,
            transcendentals=group * heads * frame_tok * keys,
        ),
        compiler_params=pltpu.CompilerParams(vmem_limit_bytes=48 * 1024 * 1024),
    )(past_bias, gains, query, own_kv, *hop_kv, bias)


def window_bias(mask_rows, tile_count):
    tile_cols = min(tile_count, 4)
    pos = jnp.arange(tile_count * TH * TW, dtype=jnp.int32)
    tile, within = pos // (TH * TW), pos % (TH * TW)
    row = (tile // tile_cols * TH + within // TW) // BLK
    col = (tile % tile_cols * TW + within % TW) // BLK
    down = row[None, :] - row[:, None]
    across = col[None, :] - col[:, None]
    near = (jnp.abs(down) <= 1) & (jnp.abs(across) <= 1)
    code = jnp.where(near, (down + 1) * 3 + across + 1, -1)
    allowed = (code == 4)[None]
    for offset in range(9):
        allowed = allowed | (code == offset)[None] & (mask_rows[:, offset] == 1)[:, None, None]
    return jnp.where(allowed, 0.0, NEG_BIG).astype(jnp.float32)


def shards(queries, keys, values, step_index, frame_index, window_mask, history_mask, step_gain):
    tile_count = lax.axis_size("tile")
    frame_count = lax.axis_size("frame")
    group = group_frames(frame_count, tile_count)
    members = group * tile_count
    head_share = HEADS // members
    frame_id = lax.axis_index("frame")
    member = (frame_id % group) * tile_count + lax.axis_index("tile")
    both = ("frame", "tile")
    teams = [
        [g * members + n for n in range(members)] for g in range(frame_count // group)
    ]
    frame_teams = [[g * group + n for n in range(group)] for g in range(frame_count // group)]

    def exchange(block):
        return lax.all_to_all(block, both, 0, 0, axis_index_groups=teams, tiled=True)

    def from_behind(block, hop):
        step = hop * group
        return lax.ppermute(
            block, "frame", [(i, i + step) for i in range(frame_count) if i + step < frame_count]
        )

    own_q, own_k, own_v = queries[0, 0], keys[0, 0], values[0, 0]

    distance = jnp.arange(1, WIN + 1, dtype=jnp.int32)
    usable = (
        (history_mask[0] == 1) & (distance <= frame_index[0]) & (frame_id - distance >= 0)
    ).astype(jnp.int32)
    facts = jnp.concatenate([usable, step_index])[None]
    if group > 1:
        facts = lax.all_gather(facts, "frame", axis_index_groups=frame_teams, tiled=True)
    past_bias = jnp.where(facts[:, :WIN] == 1, 0.0, NEG_BIG).astype(jnp.float32)
    gains = jnp.zeros((group, head_share), jnp.float32)
    my_gain = lax.dynamic_slice(step_gain, (0, member * head_share), (STEPS, head_share))
    for s in range(STEPS):
        gains = jnp.where(facts[:, WIN:] == s, my_gain[s][None], gains)
    my_mask = lax.dynamic_slice(window_mask, (member * head_share, 0), (head_share, 9))
    bias = window_bias(my_mask, tile_count)

    starts = [sum(CHUNKS[:c]) for c in range(len(CHUNKS))]
    kv = [
        exchange(pack([own_k, own_v], members, head_share, s, n)) for s, n in zip(starts, CHUNKS)
    ]
    q = [exchange(pack([own_q], members, head_share, s, n)) for s, n in zip(starts, CHUNKS)]
    parts = []
    for c, (s, n) in enumerate(zip(starts, CHUNKS)):
        hop_kv, behind, low = [], kv[c], 0
        for hop in range(1, -(-WIN // group) + 1):
            need = first_needed(hop, group)
            behind = from_behind(behind[(need - low) * tile_count :], 1)
            low = need
            hop_kv.append(behind)
        out = attend(
            q[c], kv[c], hop_kv, bias[s : s + n], past_bias, gains[:, s : s + n], group
        )
        parts.append(exchange(out))
    return unpack(parts, starts, head_share)[None, None]


def solution(mesh):
    return jax.shard_map(
        shards,
        mesh=mesh,
        in_specs=(
            P("frame", "tile", None, None),
            P("frame", "tile", None, None),
            P("frame", "tile", None, None),
            P("frame"),
            P("frame"),
            P(),
            P("frame", None),
            P(),
        ),
        out_specs=P("frame", "tile", None, None),
        check_vma=False,
    )
```

```python
import functools
import math

import jax
import jax.numpy as jnp
from jax import lax
from jax.experimental import pallas as pl
from jax.experimental.pallas import tpu as pltpu
from jax.sharding import PartitionSpec as P

HEADS = 40
HD = 128
TH = 8
TW = 8
BLK = 4
WIN = 5
STEPS = 4

NEG_BIG = -1e30
FACT_ROWS = 8

VMEM = pl.BlockSpec(memory_space=pltpu.VMEM)
SMEM = pl.BlockSpec(memory_space=pltpu.SMEM)


def team_frames(frame_count, tile_count):
    return max(
        g
        for g in range(1, frame_count + 1)
        if frame_count % g == 0 and HEADS % (g * tile_count) == 0
    )


def first_needed(hop, group):
    return max(0, hop * group - WIN)


def partner(member, m, members):
    return member ^ m if members & (members - 1) == 0 else (member + m) % members


def sender(member, m, members):
    return member ^ m if members & (members - 1) == 0 else (member - m) % members


def here(group, tiles):
    return lax.rem(lax.axis_index("frame"), group) * tiles + lax.axis_index("tile")


def pack_kv(own_k, own_v, group, tiles, head_share):
    tokens = own_k.shape[0]
    width = head_share * HD
    members = group * tiles

    def body(k_ref, v_ref, own, *outs):
        for n in range(members):
            lanes = pl.ds(n * width, width)
            own[n, :, :width] = k_ref[:, lanes]
            own[n, :, width:] = v_ref[:, lanes]
        member = here(group, tiles)
        for m, out in enumerate(outs):
            out[...] = own[partner(member, m, members)]

    shape = (tokens, 2 * width)
    return pl.pallas_call(
        body,
        out_shape=[jax.ShapeDtypeStruct((members,) + shape, jnp.bfloat16)]
        + [jax.ShapeDtypeStruct(shape, jnp.bfloat16)] * members,
        in_specs=[VMEM] * 2,
        out_specs=[VMEM] * (1 + members),
    )(own_k, own_v)


def pack_queries(history, frame_index, step_index, own_q, members):
    tokens, channels = own_q.shape
    width = channels // members

    def body(history_ref, index_ref, step_ref, q_ref, out):
        row = lax.broadcasted_iota(jnp.int32, (tokens, HD), 0)
        block = jnp.where(row == WIN, step_ref[0], 0)
        for d in range(1, WIN + 1):
            usable = (
                (history_ref[0, d - 1] == 1)
                & (d <= index_ref[0])
                & (d <= lax.axis_index("frame"))
            )
            block = jnp.where(row == d - 1, usable.astype(jnp.int32), block)
        block = block.astype(jnp.float32).astype(jnp.bfloat16)
        for n in range(members):
            out[n, :, :width] = q_ref[:, n * width : (n + 1) * width]
            out[n, :, width:] = block

    return pl.pallas_call(
        body,
        out_shape=jax.ShapeDtypeStruct((members, tokens, width + HD), jnp.bfloat16),
        in_specs=[SMEM] * 3 + [VMEM],
        out_specs=VMEM,
    )(history, frame_index, step_index, own_q)


def unpack(parts, starts, head_share):
    members, tokens = parts[0].shape[:2]

    def body(*refs):
        out = refs[-1]
        for start, ref in zip(starts, refs[:-1]):
            for n in range(members):
                out[:, pl.ds((n * head_share + start) * HD, ref.shape[-1])] = ref[n]

    return pl.pallas_call(
        body,
        out_shape=jax.ShapeDtypeStruct((tokens, members * head_share * HD), jnp.bfloat16),
        in_specs=[VMEM] * len(parts),
        out_specs=VMEM,
    )(*parts)


FACTOR = math.log2(math.e) / math.sqrt(HD)


def frame_facts(asked_ref, row, frame_tok):
    facts = asked_ref[row, :16, asked_ref.shape[-1] - HD :].astype(jnp.float32)
    past = (facts[:FACT_ROWS] - 1.0) * -NEG_BIG
    past = [past[d : d + 1] for d in range(WIN) for _ in range(frame_tok // HD)]
    return jnp.concatenate(past, axis=1), facts[WIN : WIN + 1]


def head_gain(gain_ref, step, h):
    gain = jnp.zeros((1, HD), jnp.float32)
    for s in range(STEPS):
        gain = jnp.where(step == s, gain_ref[s, h], gain)
    return gain


def rows_of(ref, row, tiles, lane):
    return ref[row : row + tiles, :, lane : lane + HD].reshape(-1, HD)


def scores_of(q, k):
    return FACTOR * lax.dot_general(
        q, k, (((1,), (1,)), ((), ())), preferred_element_type=jnp.float32
    )


def cost(pairs, frame_tok):
    return pl.CostEstimate(
        flops=4 * pairs * frame_tok * frame_tok * HD,
        bytes_accessed=4 * pairs * frame_tok * HD,
        transcendentals=pairs * frame_tok * frame_tok,
    )


def attend_near(asked, team, ahead, bias, gains, group):
    members, tokens = team.shape[:2]
    tiles = members // group
    frame_tok = tiles * tokens
    width = team.shape[-1] // 2
    heads = width // HD
    unfinished = max(0, min(group, WIN - group))

    def body(gain_ref, bias_ref, asked_ref, team_ref, *refs):
        ahead_refs = refs[:members]
        out_ref, sum_ref, top_ref, norm_ref, before_ref = refs[members:]
        member = here(group, tiles)
        for m, ref in enumerate(ahead_refs):
            before_ref[sender(member, m, members)] = ref[...]
        lane_id = lax.broadcasted_iota(jnp.int32, (frame_tok, HD), 1)
        for j in range(group):
            past, step = frame_facts(asked_ref, j * tiles, frame_tok)
            near = min(WIN, j + group)
            frames = [(team_ref, j - d) if d <= j else (before_ref, j - d + group) for d in range(near + 1)]
            tops = norms = jnp.zeros((frame_tok, HD), jnp.float32)
            for h in range(heads):
                lane = h * HD
                q = rows_of(asked_ref, j * tiles, tiles, lane)
                k = jnp.concatenate([rows_of(r, f * tiles, tiles, lane) for r, f in frames])
                v = jnp.concatenate([rows_of(r, f * tiles, tiles, width + lane) for r, f in frames])
                scores = scores_of(q, k)
                scores = jnp.concatenate(
                    [
                        scores[:, :frame_tok] + bias_ref[h],
                        scores[:, frame_tok:] + past[:, : near * frame_tok],
                    ],
                    axis=1,
                )
                top = jnp.max(scores, axis=1, keepdims=True)
                p = jnp.exp2(scores - top)
                norm = jnp.sum(p, axis=1, keepdims=True)
                blended = jnp.dot(p.astype(jnp.bfloat16), v, preferred_element_type=jnp.float32)
                if j < unfinished:
                    sum_ref[j, :, lane : lane + HD] = blended
                    tops = jnp.where(lane_id == h, top, tops)
                    norms = jnp.where(lane_id == h, norm, norms)
                else:
                    result = (blended / norm * head_gain(gain_ref, step, h)).astype(jnp.bfloat16)
                    out_ref[j * tiles : (j + 1) * tiles, :, lane : lane + HD] = result.reshape(
                        tiles, tokens, HD
                    )
            if j < unfinished:
                top_ref[j] = tops
                norm_ref[j] = norms
                out_ref[j * tiles : (j + 1) * tiles] = jnp.zeros((tiles, tokens, width), jnp.bfloat16)

    parts = max(1, unfinished)
    return pl.pallas_call(
        body,
        out_shape=[
            jax.ShapeDtypeStruct((members, tokens, width), jnp.bfloat16),
            jax.ShapeDtypeStruct((parts, frame_tok, width), jnp.float32),
            jax.ShapeDtypeStruct((parts, frame_tok, HD), jnp.float32),
            jax.ShapeDtypeStruct((parts, frame_tok, HD), jnp.float32),
        ],
        in_specs=[SMEM] + [VMEM] * (3 + members),
        out_specs=[VMEM] * 4,
        scratch_shapes=[pltpu.VMEM((members, tokens, 2 * width), jnp.bfloat16)],
        cost_estimate=cost(group * heads * (WIN + 1), frame_tok),
        compiler_params=pltpu.CompilerParams(vmem_limit_bytes=48 * 1024 * 1024),
    )(gains, bias, asked, team, *ahead)


def attend_far(asked, far, state, gains, group):
    out, sums, tops, norms = state
    members, tokens, width = out.shape
    tiles = members // group
    frame_tok = tiles * tokens
    heads = width // HD
    unfinished = min(group, WIN - group)

    def body(gain_ref, asked_ref, sum_ref, top_ref, norm_ref, near_ref, *refs):
        far_refs, out_ref = refs[:-1], refs[-1]
        if unfinished < group:
            out_ref[unfinished * tiles :] = near_ref[unfinished * tiles :]
        for j in range(unfinished):
            past, step = frame_facts(asked_ref, j * tiles, frame_tok)
            frames = []
            for d in range(j + group + 1, WIN + 1):
                hop = -((j - d) // group)
                frames.append((far_refs[hop - 2], j - d + hop * group - first_needed(hop, group)))
            for h in range(heads):
                lane = h * HD
                q = rows_of(asked_ref, j * tiles, tiles, lane)
                k = jnp.concatenate([rows_of(r, f * tiles, tiles, lane) for r, f in frames])
                v = jnp.concatenate([rows_of(r, f * tiles, tiles, width + lane) for r, f in frames])
                scores = scores_of(q, k) + past[:, (j + group) * frame_tok :]
                top = top_ref[j, :, h : h + 1]
                both = jnp.maximum(top, jnp.max(scores, axis=1, keepdims=True))
                p = jnp.exp2(scores - both)
                kept = jnp.exp2(top - both)
                norm = norm_ref[j, :, h : h + 1] * kept + jnp.sum(p, axis=1, keepdims=True)
                blended = sum_ref[j, :, lane : lane + HD] * kept + jnp.dot(
                    p.astype(jnp.bfloat16), v, preferred_element_type=jnp.float32
                )
                result = (blended / norm * head_gain(gain_ref, step, h)).astype(jnp.bfloat16)
                out_ref[j * tiles : (j + 1) * tiles, :, lane : lane + HD] = result.reshape(
                    tiles, tokens, HD
                )

    return pl.pallas_call(
        body,
        out_shape=jax.ShapeDtypeStruct(out.shape, out.dtype),
        in_specs=[SMEM] + [VMEM] * (5 + len(far)),
        out_specs=VMEM,
        cost_estimate=cost(unfinished * heads, frame_tok),
        compiler_params=pltpu.CompilerParams(vmem_limit_bytes=48 * 1024 * 1024),
    )(gains, asked, sums, tops, norms, out, *far)


def window_bias(mask_rows, tile_count):
    tile_cols = min(tile_count, 4)
    pos = jnp.arange(tile_count * TH * TW, dtype=jnp.int32)
    tile, within = pos // (TH * TW), pos % (TH * TW)
    row = (tile // tile_cols * TH + within // TW) // BLK
    col = (tile % tile_cols * TW + within % TW) // BLK
    down = row[None, :] - row[:, None]
    across = col[None, :] - col[:, None]
    near = (jnp.abs(down) <= 1) & (jnp.abs(across) <= 1)
    code = jnp.where(near, (down + 1) * 3 + across + 1, -1)
    allowed = (code == 4)[None]
    for offset in range(9):
        allowed = allowed | (code == offset)[None] & (mask_rows[:, offset] == 1)[:, None, None]
    return jnp.where(allowed, 0.0, NEG_BIG).astype(jnp.float32)


def shards(queries, keys, values, step_index, frame_index, window_mask, history_mask, step_gain):
    tile_count = lax.axis_size("tile")
    frame_count = lax.axis_size("frame")
    group = team_frames(frame_count, tile_count)
    members = group * tile_count
    teams = frame_count // group
    head_share = HEADS // members
    hops = -(-WIN // group)
    both = ("frame", "tile")

    def exchange(block):
        return lax.all_to_all(
            block,
            both,
            0,
            0,
            axis_index_groups=[[t * members + n for n in range(members)] for t in range(teams)],
            tiled=True,
        )

    def team_permute(block, ahead, m):
        route = [
            (t * members + n, (t + ahead) % teams * members + partner(n, m, members))
            for t in range(teams)
            for n in range(members)
        ]
        return lax.ppermute(block, both, route)

    packed_kv, *ahead = pack_kv(keys[0, 0], values[0, 0], group, tile_count, head_share)
    ahead = [team_permute(block, 1, m) for m, block in enumerate(ahead)]
    team = exchange(packed_kv)
    team, ahead[:4] = lax.optimization_barrier((team, ahead[:4]))
    far = [
        team_permute(team[first_needed(hop, group) * tile_count :], hop, 0)
        for hop in range(2, hops + 1)
    ]
    asked = pack_queries(history_mask, frame_index, step_index, queries[0, 0], members)
    asked, ahead[2] = lax.optimization_barrier((asked, ahead[2]))
    asked = exchange(asked)

    share = here(group, tile_count) * head_share
    gains = lax.dynamic_slice(step_gain, (0, share), (STEPS, head_share))
    my_mask = lax.dynamic_slice(window_mask, (share, 0), (head_share, 9))
    bias = window_bias(my_mask, tile_count)
    state = attend_near(asked, team, ahead, bias, gains, group)
    out = attend_far(asked, far, state, gains, group) if far else state[0]
    return unpack([exchange(out)], [0], head_share)[None, None]


def solution(mesh):
    return jax.shard_map(
        shards,
        mesh=mesh,
        in_specs=(
            P("frame", "tile", None, None),
            P("frame", "tile", None, None),
            P("frame", "tile", None, None),
            P("frame"),
            P("frame"),
            P(),
            P("frame", None),
            P(),
        ),
        out_specs=P("frame", "tile", None, None),
        check_vma=False,
    )
```

```python
import functools
import math

import jax
import jax.numpy as jnp
from jax import lax
from jax.experimental import pallas as pl
from jax.experimental.pallas import tpu as pltpu
from jax.sharding import PartitionSpec as P

HEADS = 40
HD = 128
TH = 8
TW = 8
BLK = 4
WIN = 5
STEPS = 4

NEG_BIG = -1e30
FACT_ROWS = 8

VMEM = pl.BlockSpec(memory_space=pltpu.VMEM)
SMEM = pl.BlockSpec(memory_space=pltpu.SMEM)


def team_frames(frame_count, tile_count):
    return max(
        g
        for g in range(1, frame_count + 1)
        if frame_count % g == 0 and HEADS % (g * tile_count) == 0
    )


def first_needed(hop, group):
    return max(0, hop * group - WIN)


def partner(member, m, members):
    return member ^ m if members & (members - 1) == 0 else (member + m) % members


def sender(member, m, members):
    return member ^ m if members & (members - 1) == 0 else (member - m) % members


def here(group, tiles):
    return lax.rem(lax.axis_index("frame"), group) * tiles + lax.axis_index("tile")


def pack_kv(own_k, own_v, group, tiles, head_share):
    tokens = own_k.shape[0]
    width = head_share * HD
    members = group * tiles

    def body(k_ref, v_ref, own, *outs):
        for n in range(members):
            lanes = pl.ds(n * width, width)
            own[n, :, :width] = k_ref[:, lanes]
            own[n, :, width:] = v_ref[:, lanes]
        member = here(group, tiles)
        for m, out in enumerate(outs):
            out[...] = own[partner(member, m, members)]

    shape = (tokens, 2 * width)
    return pl.pallas_call(
        body,
        out_shape=[jax.ShapeDtypeStruct((members,) + shape, jnp.bfloat16)]
        + [jax.ShapeDtypeStruct(shape, jnp.bfloat16)] * members,
        in_specs=[VMEM] * 2,
        out_specs=[VMEM] * (1 + members),
    )(own_k, own_v)


def pack_queries(history, frame_index, step_index, own_q, members):
    tokens, channels = own_q.shape
    width = channels // members

    def body(history_ref, index_ref, step_ref, q_ref, out):
        row = lax.broadcasted_iota(jnp.int32, (tokens, HD), 0)
        block = jnp.where(row == WIN, step_ref[0], 0)
        for d in range(1, WIN + 1):
            usable = (
                (history_ref[0, d - 1] == 1)
                & (d <= index_ref[0])
                & (d <= lax.axis_index("frame"))
            )
            block = jnp.where(row == d - 1, usable.astype(jnp.int32), block)
        block = block.astype(jnp.float32).astype(jnp.bfloat16)
        for n in range(members):
            out[n, :, :width] = q_ref[:, n * width : (n + 1) * width]
            out[n, :, width:] = block

    return pl.pallas_call(
        body,
        out_shape=jax.ShapeDtypeStruct((members, tokens, width + HD), jnp.bfloat16),
        in_specs=[SMEM] * 3 + [VMEM],
        out_specs=VMEM,
    )(history, frame_index, step_index, own_q)


def unpack(parts, starts, head_share):
    members, tokens = parts[0].shape[:2]

    def body(*refs):
        out = refs[-1]
        for start, ref in zip(starts, refs[:-1]):
            for n in range(members):
                out[:, pl.ds((n * head_share + start) * HD, ref.shape[-1])] = ref[n]

    return pl.pallas_call(
        body,
        out_shape=jax.ShapeDtypeStruct((tokens, members * head_share * HD), jnp.bfloat16),
        in_specs=[VMEM] * len(parts),
        out_specs=VMEM,
    )(*parts)


FACTOR = math.log2(math.e) / math.sqrt(HD)


def frame_facts(asked_ref, row, frame_tok):
    facts = asked_ref[row, :16, asked_ref.shape[-1] - HD :].astype(jnp.float32)
    past = (facts[:FACT_ROWS] - 1.0) * -NEG_BIG
    past = [past[d : d + 1] for d in range(WIN) for _ in range(frame_tok // HD)]
    return jnp.concatenate(past, axis=1), facts[WIN : WIN + 1]


def head_gain(gain_ref, step, h):
    gain = jnp.zeros((1, HD), jnp.float32)
    for s in range(STEPS):
        gain = jnp.where(step == s, gain_ref[s, h], gain)
    return gain


def rows_of(ref, row, tiles, lane):
    return ref[row : row + tiles, :, lane : lane + HD].reshape(-1, HD)


def scores_of(q, k):
    return FACTOR * lax.dot_general(
        q, k, (((1,), (1,)), ((), ())), preferred_element_type=jnp.float32
    )


def weigh(weights, v):
    v = jnp.concatenate([v, jnp.ones(v.shape, v.dtype)], axis=1)
    both = jnp.dot(weights.astype(jnp.bfloat16), v, preferred_element_type=jnp.float32)
    return both[:, :HD], both[:, HD:]


def cost(pairs, frame_tok):
    return pl.CostEstimate(
        flops=4 * pairs * frame_tok * frame_tok * HD,
        bytes_accessed=4 * pairs * frame_tok * HD,
        transcendentals=pairs * frame_tok * frame_tok,
    )


def attend_near(asked, team, ahead, bias, gains, group):
    members, tokens = team.shape[:2]
    tiles = members // group
    frame_tok = tiles * tokens
    width = team.shape[-1] // 2
    heads = width // HD
    unfinished = max(0, min(group, WIN - group))

    def body(gain_ref, bias_ref, asked_ref, team_ref, *refs):
        ahead_refs = refs[:members]
        out_ref, sum_ref, top_ref, norm_ref, before_ref = refs[members:]
        member = here(group, tiles)
        for m, ref in enumerate(ahead_refs):
            before_ref[sender(member, m, members)] = ref[...]
        lane_id = lax.broadcasted_iota(jnp.int32, (frame_tok, HD), 1)
        for j in range(group):
            past, step = frame_facts(asked_ref, j * tiles, frame_tok)
            near = min(WIN, j + group)
            frames = [(team_ref, j - d) if d <= j else (before_ref, j - d + group) for d in range(near + 1)]
            tops = norms = jnp.zeros((frame_tok, HD), jnp.float32)
            for h in range(heads):
                lane = h * HD
                q = rows_of(asked_ref, j * tiles, tiles, lane)
                k = jnp.concatenate([rows_of(r, f * tiles, tiles, lane) for r, f in frames])
                v = jnp.concatenate([rows_of(r, f * tiles, tiles, width + lane) for r, f in frames])
                scores = scores_of(q, k)
                scores = jnp.concatenate(
                    [
                        scores[:, :frame_tok] + bias_ref[h],
                        scores[:, frame_tok:] + past[:, : near * frame_tok],
                    ],
                    axis=1,
                )
                top = jnp.max(scores, axis=1, keepdims=True)
                p = jnp.exp2(scores - top)
                blended, norm = weigh(p, v)
                if j < unfinished:
                    sum_ref[j, :, lane : lane + HD] = blended
                    tops = jnp.where(lane_id == h, top, tops)
                    norms = jnp.where(lane_id == h, norm, norms)
                else:
                    result = (blended / norm * head_gain(gain_ref, step, h)).astype(jnp.bfloat16)
                    out_ref[j * tiles : (j + 1) * tiles, :, lane : lane + HD] = result.reshape(
                        tiles, tokens, HD
                    )
            if j < unfinished:
                top_ref[j] = tops
                norm_ref[j] = norms

    parts = max(1, unfinished)
    return pl.pallas_call(
        body,
        out_shape=[
            jax.ShapeDtypeStruct((members, tokens, width), jnp.bfloat16),
            jax.ShapeDtypeStruct((parts, frame_tok, width), jnp.float32),
            jax.ShapeDtypeStruct((parts, frame_tok, HD), jnp.float32),
            jax.ShapeDtypeStruct((parts, frame_tok, HD), jnp.float32),
        ],
        in_specs=[SMEM] + [VMEM] * (3 + members),
        out_specs=[VMEM] * 4,
        scratch_shapes=[pltpu.VMEM((members, tokens, 2 * width), jnp.bfloat16)],
        cost_estimate=cost(group * heads * (WIN + 1), frame_tok),
        compiler_params=pltpu.CompilerParams(vmem_limit_bytes=48 * 1024 * 1024),
    )(gains, bias, asked, team, *ahead)


def attend_far(asked, far, state, gains, group):
    out, sums, tops, norms = state
    members, tokens, width = out.shape
    tiles = members // group
    frame_tok = tiles * tokens
    heads = width // HD
    unfinished = min(group, WIN - group)

    def body(gain_ref, asked_ref, sum_ref, top_ref, norm_ref, near_ref, *refs):
        far_refs, out_ref = refs[:-1], refs[-1]
        for j in range(unfinished):
            past, step = frame_facts(asked_ref, j * tiles, frame_tok)
            frames = []
            for d in range(j + group + 1, WIN + 1):
                hop = -((j - d) // group)
                frames.append((far_refs[hop - 2], j - d + hop * group - first_needed(hop, group)))
            for h in range(heads):
                lane = h * HD
                q = rows_of(asked_ref, j * tiles, tiles, lane)
                k = jnp.concatenate([rows_of(r, f * tiles, tiles, lane) for r, f in frames])
                v = jnp.concatenate([rows_of(r, f * tiles, tiles, width + lane) for r, f in frames])
                scores = scores_of(q, k) + past[:, (j + group) * frame_tok :]
                top = top_ref[j, :, h : h + 1]
                both = jnp.maximum(top, jnp.max(scores, axis=1, keepdims=True))
                blended, norm = weigh(jnp.exp2(scores - both), v)
                kept = jnp.exp2(top - both)
                blended += sum_ref[j, :, lane : lane + HD] * kept
                norm += norm_ref[j, :, h : h + 1] * kept
                result = (blended / norm * head_gain(gain_ref, step, h)).astype(jnp.bfloat16)
                out_ref[j * tiles : (j + 1) * tiles, :, lane : lane + HD] = result.reshape(
                    tiles, tokens, HD
                )

    def leading(array):
        return pl.BlockSpec((unfinished * tiles,) + array.shape[1:], lambda i: (0, 0, 0))

    return pl.pallas_call(
        body,
        grid=(1,),
        out_shape=jax.ShapeDtypeStruct(out.shape, out.dtype),
        in_specs=[SMEM, leading(asked)]
        + [VMEM] * 3
        + [pl.BlockSpec(memory_space=pl.ANY)]
        + [VMEM] * len(far),
        out_specs=leading(out),
        input_output_aliases={5: 0},
        cost_estimate=cost(unfinished * heads, frame_tok),
        compiler_params=pltpu.CompilerParams(vmem_limit_bytes=48 * 1024 * 1024),
    )(gains, asked, sums, tops, norms, out, *far)


def window_bias(mask_rows, tile_count):
    tile_cols = min(tile_count, 4)
    pos = jnp.arange(tile_count * TH * TW, dtype=jnp.int32)
    tile, within = pos // (TH * TW), pos % (TH * TW)
    row = (tile // tile_cols * TH + within // TW) // BLK
    col = (tile % tile_cols * TW + within % TW) // BLK
    down = row[None, :] - row[:, None]
    across = col[None, :] - col[:, None]
    near = (jnp.abs(down) <= 1) & (jnp.abs(across) <= 1)
    code = jnp.where(near, (down + 1) * 3 + across + 1, -1)
    allowed = (code == 4)[None]
    for offset in range(9):
        allowed = allowed | (code == offset)[None] & (mask_rows[:, offset] == 1)[:, None, None]
    return jnp.where(allowed, 0.0, NEG_BIG).astype(jnp.float32)


def shards(queries, keys, values, step_index, frame_index, window_mask, history_mask, step_gain):
    tile_count = lax.axis_size("tile")
    frame_count = lax.axis_size("frame")
    group = team_frames(frame_count, tile_count)
    members = group * tile_count
    teams = frame_count // group
    head_share = HEADS // members
    hops = -(-WIN // group)
    both = ("frame", "tile")

    def exchange(block):
        return lax.all_to_all(
            block,
            both,
            0,
            0,
            axis_index_groups=[[t * members + n for n in range(members)] for t in range(teams)],
            tiled=True,
        )

    def team_permute(block, ahead, m):
        route = [
            (t * members + n, (t + ahead) % teams * members + partner(n, m, members))
            for t in range(teams)
            for n in range(members)
        ]
        return lax.ppermute(block, both, route)

    packed_kv, *ahead = pack_kv(keys[0, 0], values[0, 0], group, tile_count, head_share)
    sent = {}
    for m in [0, 2, 1, 3, 4, 6, 5, 7]:
        block = ahead[m]
        sent[m] = team_permute(block, 1, m)
    ahead = [sent[m] for m in range(members)]
    team = exchange(packed_kv)
    team, *some = lax.optimization_barrier((team, *[ahead[m] for m in [0, 2, 1, 3]]))
    for m, block in zip([0, 2, 1, 3], some):
        ahead[m] = block
    far = [
        team_permute(team[first_needed(hop, group) * tile_count :], hop, 0)
        for hop in range(2, hops + 1)
    ]
    asked = pack_queries(history_mask, frame_index, step_index, queries[0, 0], members)
    asked, *some = lax.optimization_barrier((asked, *[ahead[m] for m in [1]]))
    for m, block in zip([1], some):
        ahead[m] = block
    asked = exchange(asked)

    share = here(group, tile_count) * head_share
    gains = lax.dynamic_slice(step_gain, (0, share), (STEPS, head_share))
    my_mask = lax.dynamic_slice(window_mask, (share, 0), (head_share, 9))
    bias = window_bias(my_mask, tile_count)
    state = attend_near(asked, team, ahead, bias, gains, group)
    out = attend_far(asked, far, state, gains, group) if far else state[0]
    return unpack([exchange(out)], [0], head_share)[None, None]


def solution(mesh):
    return jax.shard_map(
        shards,
        mesh=mesh,
        in_specs=(
            P("frame", "tile", None, None),
            P("frame", "tile", None, None),
            P("frame", "tile", None, None),
            P("frame"),
            P("frame"),
            P(),
            P("frame", None),
            P(),
        ),
        out_specs=P("frame", "tile", None, None),
        check_vma=False,
    )
```

```python
import functools
import math

import jax
import jax.numpy as jnp
from jax import lax
from jax.experimental import pallas as pl
from jax.experimental.pallas import tpu as pltpu
from jax.sharding import PartitionSpec as P

HEADS = 40
HD = 128
TH = 8
TW = 8
BLK = 4
WIN = 5
STEPS = 4

NEG_BIG = -1e30
FACT_ROWS = 8

VMEM = pl.BlockSpec(memory_space=pltpu.VMEM)
SMEM = pl.BlockSpec(memory_space=pltpu.SMEM)


def team_frames(frame_count, tile_count):
    return max(
        g
        for g in range(1, frame_count + 1)
        if frame_count % g == 0 and HEADS % (g * tile_count) == 0
    )


def first_needed(hop, group):
    return max(0, hop * group - WIN)


def partner(member, m, members):
    return member ^ m if members & (members - 1) == 0 else (member + m) % members


def sender(member, m, members):
    return member ^ m if members & (members - 1) == 0 else (member - m) % members


def here(group, tiles):
    return lax.rem(lax.axis_index("frame"), group) * tiles + lax.axis_index("tile")


def pack_kv(own_k, own_v, group, tiles, head_share):
    tokens = own_k.shape[0]
    width = head_share * HD
    members = group * tiles

    def body(k_ref, v_ref, own, *outs):
        for n in range(members):
            lanes = pl.ds(n * width, width)
            own[n, :, :width] = k_ref[:, lanes]
            own[n, :, width:] = v_ref[:, lanes]
        member = here(group, tiles)
        for m, out in enumerate(outs):
            out[...] = own[partner(member, m, members)]

    shape = (tokens, 2 * width)
    return pl.pallas_call(
        body,
        out_shape=[jax.ShapeDtypeStruct((members,) + shape, jnp.bfloat16)]
        + [jax.ShapeDtypeStruct(shape, jnp.bfloat16)] * members,
        in_specs=[VMEM] * 2,
        out_specs=[VMEM] * (1 + members),
    )(own_k, own_v)


def pack_queries(history, frame_index, step_index, own_q, members):
    tokens, channels = own_q.shape
    width = channels // members

    def body(history_ref, index_ref, step_ref, q_ref, out):
        row = lax.broadcasted_iota(jnp.int32, (tokens, HD), 0)
        block = jnp.where(row == WIN, step_ref[0], 0)
        for d in range(1, WIN + 1):
            usable = (
                (history_ref[0, d - 1] == 1)
                & (d <= index_ref[0])
                & (d <= lax.axis_index("frame"))
            )
            block = jnp.where(row == d - 1, usable.astype(jnp.int32), block)
        block = block.astype(jnp.float32).astype(jnp.bfloat16)
        for n in range(members):
            out[n, :, :width] = q_ref[:, n * width : (n + 1) * width]
            out[n, :, width:] = block

    return pl.pallas_call(
        body,
        out_shape=jax.ShapeDtypeStruct((members, tokens, width + HD), jnp.bfloat16),
        in_specs=[SMEM] * 3 + [VMEM],
        out_specs=VMEM,
    )(history, frame_index, step_index, own_q)


def unpack(blocks, group, tiles, order):
    members = len(blocks)
    tokens, width = blocks[0].shape

    def body(*refs):
        member = here(group, tiles)
        for m, ref in zip(order, refs[:-1]):
            lanes = pl.multiple_of(sender(member, m, members) * width, HD)
            refs[-1][:, pl.ds(lanes, width)] = ref[...]

    return pl.pallas_call(
        body,
        out_shape=jax.ShapeDtypeStruct((tokens, members * width), jnp.bfloat16),
        in_specs=[VMEM] * members,
        out_specs=VMEM,
        compiler_params=pltpu.CompilerParams(vmem_limit_bytes=16 * 1024 * 1024),
    )(*[blocks[m] for m in order])


FACTOR = math.log2(math.e) / math.sqrt(HD)


def frame_facts(asked_ref, row, frame_tok):
    facts = asked_ref[row, :16, asked_ref.shape[-1] - HD :].astype(jnp.float32)
    past = (facts[:FACT_ROWS] - 1.0) * -NEG_BIG
    past = [past[d : d + 1] for d in range(WIN) for _ in range(frame_tok // HD)]
    return jnp.concatenate(past, axis=1), facts[WIN : WIN + 1]


def head_gain(gain_ref, step, h):
    gain = jnp.zeros((1, HD), jnp.float32)
    for s in range(STEPS):
        gain = jnp.where(step == s, gain_ref[s, h], gain)
    return gain


def rows_of(ref, row, tiles, lane):
    return ref[row : row + tiles, :, lane : lane + HD].reshape(-1, HD)


def scores_of(q, k):
    return FACTOR * lax.dot_general(
        q, k, (((1,), (1,)), ((), ())), preferred_element_type=jnp.float32
    )


def weigh(weights, v):
    v = jnp.concatenate([v, jnp.ones(v.shape, v.dtype)], axis=1)
    both = jnp.dot(weights.astype(jnp.bfloat16), v, preferred_element_type=jnp.float32)
    return both[:, :HD], both[:, HD:]


def cost(pairs, frame_tok):
    return pl.CostEstimate(
        flops=4 * pairs * frame_tok * frame_tok * HD,
        bytes_accessed=4 * pairs * frame_tok * HD,
        transcendentals=pairs * frame_tok * frame_tok,
    )


def put_frame(out_ref, j, group, gain_ref, bias_ref, asked_ref, team_ref, before_ref, far_refs):
    members, tokens, width = out_ref.shape
    tiles = members // group
    frame_tok = tiles * tokens
    past, step = frame_facts(asked_ref, j * tiles, frame_tok)
    frames = []
    for d in range(WIN + 1):
        hop = max(0, -((j - d) // group))
        ref = (team_ref, before_ref, *far_refs)[hop]
        skipped = first_needed(hop, group) if hop > 1 else 0
        frames.append((ref, (j - d + hop * group - skipped) * tiles))
    for h in range(width // HD):
        lane = h * HD
        q = rows_of(asked_ref, j * tiles, tiles, lane)
        k = jnp.concatenate([rows_of(r, row, tiles, lane) for r, row in frames])
        v = jnp.concatenate([rows_of(r, row, tiles, width + lane) for r, row in frames])
        scores = scores_of(q, k)
        scores = jnp.concatenate(
            [scores[:, :frame_tok] + bias_ref[h], scores[:, frame_tok:] + past], axis=1
        )
        weights = jnp.exp2(scores - jnp.max(scores, axis=1, keepdims=True))
        blended, norm = weigh(weights, v)
        result = (blended / norm * head_gain(gain_ref, step, h)).astype(jnp.bfloat16)
        out_ref[j * tiles : (j + 1) * tiles, :, lane : lane + HD] = result.reshape(
            tiles, tokens, HD
        )


def attend_near(asked, team, ahead, bias, gains, group):
    members, tokens = team.shape[:2]
    width = team.shape[-1] // 2

    def body(gain_ref, bias_ref, asked_ref, team_ref, *refs):
        out_ref, before_ref = refs[members:]
        member = here(group, members // group)
        for m, ref in enumerate(refs[:members]):
            before_ref[sender(member, m, members)] = ref[...]
        for j in range(min(group, max(0, WIN - group)), group):
            put_frame(out_ref, j, group, gain_ref, bias_ref, asked_ref, team_ref, before_ref, [])

    return pl.pallas_call(
        body,
        out_shape=[
            jax.ShapeDtypeStruct((members, tokens, width), jnp.bfloat16),
            jax.ShapeDtypeStruct(team.shape, jnp.bfloat16),
        ],
        in_specs=[SMEM] + [VMEM] * (3 + members),
        out_specs=[VMEM] * 2,
        cost_estimate=cost(group * width // HD * (WIN + 1), members // group * tokens),
        compiler_params=pltpu.CompilerParams(vmem_limit_bytes=48 * 1024 * 1024),
    )(gains, bias, asked, team, *ahead)


def attend_far(asked, team, before, far, near, bias, gains, group):
    members, tokens, width = near.shape
    finished = min(group, max(0, WIN - group)) * members // group

    def body(gain_ref, bias_ref, asked_ref, team_ref, before_ref, near_ref, *refs):
        far_refs, outs, all_ref = refs[: len(far)], refs[len(far) : -1], refs[-1]
        if finished < members:
            all_ref[finished:] = near_ref[finished:]
        for j in range(finished * group // members):
            put_frame(
                all_ref, j, group, gain_ref, bias_ref, asked_ref, team_ref, before_ref, far_refs
            )
        member = here(group, members // group)
        for m, out in enumerate(outs):
            out[...] = all_ref[partner(member, m, members)]

    return pl.pallas_call(
        body,
        out_shape=[jax.ShapeDtypeStruct((tokens, width), near.dtype)] * members,
        in_specs=[SMEM] + [VMEM] * (5 + len(far)),
        out_specs=[VMEM] * members,
        scratch_shapes=[pltpu.VMEM(near.shape, near.dtype)],
        cost_estimate=cost(width // HD * (WIN + 1), members // group * tokens),
        compiler_params=pltpu.CompilerParams(vmem_limit_bytes=48 * 1024 * 1024),
    )(gains, bias, asked, team, before, near, *far)


def window_bias(mask_rows, tile_count):
    tile_cols = min(tile_count, 4)
    pos = jnp.arange(tile_count * TH * TW, dtype=jnp.int32)
    tile, within = pos // (TH * TW), pos % (TH * TW)
    row = (tile // tile_cols * TH + within // TW) // BLK
    col = (tile % tile_cols * TW + within % TW) // BLK
    down = row[None, :] - row[:, None]
    across = col[None, :] - col[:, None]
    near = (jnp.abs(down) <= 1) & (jnp.abs(across) <= 1)
    code = jnp.where(near, (down + 1) * 3 + across + 1, -1)
    allowed = (code == 4)[None]
    for offset in range(9):
        allowed = allowed | (code == offset)[None] & (mask_rows[:, offset] == 1)[:, None, None]
    return jnp.where(allowed, 0.0, NEG_BIG).astype(jnp.float32)


def shards(queries, keys, values, step_index, frame_index, window_mask, history_mask, step_gain):
    tile_count = lax.axis_size("tile")
    frame_count = lax.axis_size("frame")
    group = team_frames(frame_count, tile_count)
    members = group * tile_count
    teams = frame_count // group
    head_share = HEADS // members
    hops = -(-WIN // group)
    both = ("frame", "tile")

    def exchange(block):
        return lax.all_to_all(
            block,
            both,
            0,
            0,
            axis_index_groups=[[t * members + n for n in range(members)] for t in range(teams)],
            tiled=True,
        )

    def team_permute(block, ahead, m):
        route = [
            (t * members + n, (t + ahead) % teams * members + partner(n, m, members))
            for t in range(teams)
            for n in range(members)
        ]
        return lax.ppermute(block, both, route)

    packed_kv, *ahead = pack_kv(keys[0, 0], values[0, 0], group, tile_count, head_share)
    sent = {}
    for m in [0, 2, 1, 3, 4, 6, 5, 7]:
        block = ahead[m]
        sent[m] = team_permute(block, 1, m)
    ahead = [sent[m] for m in range(members)]
    team = exchange(packed_kv)
    team, *some = lax.optimization_barrier((team, *[ahead[m] for m in [0, 2, 1, 3]]))
    for m, block in zip([0, 2, 1, 3], some):
        ahead[m] = block
    far = [
        team_permute(team[first_needed(hop, group) * tile_count :], hop, 0)
        for hop in range(2, hops + 1)
    ]
    asked = pack_queries(history_mask, frame_index, step_index, queries[0, 0], members)
    asked, *some = lax.optimization_barrier((asked, *[ahead[m] for m in [1]]))
    for m, block in zip([1], some):
        ahead[m] = block
    asked = exchange(asked)

    share = here(group, tile_count) * head_share
    gains = lax.dynamic_slice(step_gain, (0, share), (STEPS, head_share))
    my_mask = lax.dynamic_slice(window_mask, (share, 0), (head_share, 9))
    bias = window_bias(my_mask, tile_count)
    near, before = attend_near(asked, team, ahead, bias, gains, group)
    out = attend_far(asked, team, before, far, near, bias, gains, group)
    order = [4, 5, 6, 7, 1, 3, 2, 0]
    back = {m: team_permute(out[m], 0, m) if m else out[m] for m in order}
    return unpack(back, group, tile_count, order)[None, None]


def solution(mesh):
    return jax.shard_map(
        shards,
        mesh=mesh,
        in_specs=(
            P("frame", "tile", None, None),
            P("frame", "tile", None, None),
            P("frame", "tile", None, None),
            P("frame"),
            P("frame"),
            P(),
            P("frame", None),
            P(),
        ),
        out_specs=P("frame", "tile", None, None),
        check_vma=False,
    )
```

```python
import functools
import math

import jax
import jax.numpy as jnp
from jax import lax
from jax.experimental import pallas as pl
from jax.experimental.pallas import tpu as pltpu
from jax.sharding import PartitionSpec as P

HEADS = 40
HD = 128
TH = 8
TW = 8
BLK = 4
WIN = 5
STEPS = 4

NEG_BIG = -1e30
FACT_ROWS = 8
STRAIGHT = 3

VMEM = pl.BlockSpec(memory_space=pltpu.VMEM)
SMEM = pl.BlockSpec(memory_space=pltpu.SMEM)


def team_frames(frame_count, tile_count):
    return max(
        g
        for g in range(1, frame_count + 1)
        if frame_count % g == 0 and HEADS % (g * tile_count) == 0
    )


def first_needed(hop, group):
    return max(0, hop * group - WIN)


def partner(member, m, members):
    return member ^ m if members & (members - 1) == 0 else (member + m) % members


def sender(member, m, members):
    return member ^ m if members & (members - 1) == 0 else (member - m) % members


def here(group, tiles):
    return lax.rem(lax.axis_index("frame"), group) * tiles + lax.axis_index("tile")


def pack_kv(own_k, own_v, group, tiles, head_share):
    tokens = own_k.shape[0]
    width = head_share * HD
    members = group * tiles

    def body(k_ref, v_ref, own, *outs):
        cut = STRAIGHT * HD
        for n in range(members):
            first, last = n * width, (n + 1) * width
            own[n, :, :cut] = k_ref[:, first : first + cut]
            own[n, :, cut : 2 * cut] = v_ref[:, first : first + cut]
            own[n, :, 2 * cut : width + cut] = k_ref[:, first + cut : last]
            own[n, :, width + cut :] = v_ref[:, first + cut : last]
        member = here(group, tiles)
        for m, out in enumerate(outs):
            out[...] = own[partner(member, m, members)]

    shape = (tokens, 2 * width)
    return pl.pallas_call(
        body,
        out_shape=[jax.ShapeDtypeStruct((members,) + shape, jnp.bfloat16)]
        + [jax.ShapeDtypeStruct(shape, jnp.bfloat16)] * members,
        in_specs=[VMEM] * 2,
        out_specs=[VMEM] * (1 + members),
    )(own_k, own_v)


def pick_tail(blocks, group, tiles):
    members = len(blocks)
    needed = first_needed(2, group) * tiles
    cut = 2 * STRAIGHT * HD

    def body(*refs):
        member = here(group, tiles)
        for m, ref in enumerate(refs[:-1]):
            place = sender(member, m, members) - needed

            @pl.when(place >= 0)
            def _():
                refs[-1][place] = ref[:, cut:]

    tokens, width = blocks[0].shape
    return pl.pallas_call(
        body,
        out_shape=jax.ShapeDtypeStruct((members - needed, tokens, width - cut), jnp.bfloat16),
        in_specs=[VMEM] * members,
        out_specs=VMEM,
        compiler_params=pltpu.CompilerParams(vmem_limit_bytes=16 * 1024 * 1024),
    )(*blocks)


def pack_queries(history, frame_index, step_index, own_q, members):
    tokens, channels = own_q.shape
    width = channels // members

    def body(history_ref, index_ref, step_ref, q_ref, out, fact_ref):
        row = lax.broadcasted_iota(jnp.int32, fact_ref.shape, 0)
        block = jnp.where(row == WIN, step_ref[0], 0)
        for d in range(1, WIN + 1):
            usable = (
                (history_ref[0, d - 1] == 1)
                & (d <= index_ref[0])
                & (d <= lax.axis_index("frame"))
            )
            block = jnp.where(row == d - 1, usable.astype(jnp.int32), block)
        fact_ref[...] = block.astype(jnp.float32)
        for n in range(members):
            out[n] = q_ref[:, n * width : (n + 1) * width]

    return pl.pallas_call(
        body,
        out_shape=[
            jax.ShapeDtypeStruct((members, tokens, width), jnp.bfloat16),
            jax.ShapeDtypeStruct((FACT_ROWS, HD), jnp.float32),
        ],
        in_specs=[SMEM] * 3 + [VMEM],
        out_specs=[VMEM] * 2,
    )(history, frame_index, step_index, own_q)


def unpack(blocks, group, tiles, order):
    members = len(blocks)
    tokens, width = blocks[0].shape

    def body(*refs):
        member = here(group, tiles)
        for m, ref in zip(order, refs[:-1]):
            lanes = pl.multiple_of(sender(member, m, members) * width, HD)
            refs[-1][:, pl.ds(lanes, width)] = ref[...]

    return pl.pallas_call(
        body,
        out_shape=jax.ShapeDtypeStruct((tokens, members * width), jnp.bfloat16),
        in_specs=[VMEM] * members,
        out_specs=VMEM,
        compiler_params=pltpu.CompilerParams(vmem_limit_bytes=16 * 1024 * 1024),
    )(*[blocks[m] for m in order])


FACTOR = math.log2(math.e) / math.sqrt(HD)


def frame_facts(facts, frame_tok):
    past = (facts - 1.0) * -NEG_BIG
    past = [past[d : d + 1] for d in range(WIN) for _ in range(frame_tok // HD)]
    return jnp.concatenate(past, axis=1), facts[WIN : WIN + 1]


def head_gain(gain_ref, step, h):
    gain = jnp.zeros((1, HD), jnp.float32)
    for s in range(STEPS):
        gain = jnp.where(step == s, gain_ref[s, h], gain)
    return gain


def kv_lanes(h, heads, straight=STRAIGHT):
    if h < straight:
        return h * HD, (straight + h) * HD
    return (straight + h) * HD, (heads + h) * HD


def rows_of(ref, row, tiles, lane):
    return ref[row : row + tiles, :, lane : lane + HD].reshape(-1, HD)


def scores_of(q, k):
    return FACTOR * lax.dot_general(
        q, k, (((1,), (1,)), ((), ())), preferred_element_type=jnp.float32
    )


def weigh(weights, v):
    v = jnp.concatenate([v, jnp.ones(v.shape, v.dtype)], axis=1)
    both = jnp.dot(weights.astype(jnp.bfloat16), v, preferred_element_type=jnp.float32)
    return both[:, :HD], both[:, HD:]


def cost(pairs, frame_tok):
    return pl.CostEstimate(
        flops=4 * pairs * frame_tok * frame_tok * HD,
        bytes_accessed=4 * pairs * frame_tok * HD,
        transcendentals=pairs * frame_tok * frame_tok,
    )


def put_frame(
    out_ref, j, group, gain_ref, bias_ref, fact_ref, asked_ref, team_ref, before_ref, far_refs
):
    members, tokens, width = out_ref.shape
    tiles = members // group
    frame_tok = tiles * tokens
    past, step = frame_facts(fact_ref[j], frame_tok)
    frames = []
    for d in range(WIN + 1):
        hop = max(0, -((j - d) // group))
        skipped = first_needed(hop, group) if hop > 1 else 0
        frames.append((hop, (j - d + hop * group - skipped) * tiles))
    for h in range(width // HD):
        lane = h * HD
        q = rows_of(asked_ref, j * tiles, tiles, lane)
        straight = h < STRAIGHT
        refs = [team_ref, before_ref, *far_refs[int(not straight) :: 2]]
        shift = 0 if straight else 2 * STRAIGHT * HD
        k, v = (
            jnp.concatenate(
                [rows_of(refs[hop], row, tiles, at - shift * (hop > 1)) for hop, row in frames]
            )
            for at in kv_lanes(h, width // HD)
        )
        scores = scores_of(q, k)
        scores = jnp.concatenate(
            [scores[:, :frame_tok] + bias_ref[h], scores[:, frame_tok:] + past], axis=1
        )
        weights = jnp.exp2(scores - jnp.max(scores, axis=1, keepdims=True))
        blended, norm = weigh(weights, v)
        result = (blended / norm * head_gain(gain_ref, step, h)).astype(jnp.bfloat16)
        out_ref[j * tiles : (j + 1) * tiles, :, lane : lane + HD] = result.reshape(
            tiles, tokens, HD
        )


def attend_near(facts, asked, team, ahead, bias, gains, group):
    members, tokens = team.shape[:2]
    width = team.shape[-1] // 2

    tiles = members // group

    def body(gain_ref, bias_ref, asked_ref, team_ref, *refs):
        out_ref, before_ref, fact_ref = refs[members + group :]
        member = here(group, tiles)
        for m, ref in enumerate(refs[:members]):
            before_ref[sender(member, m, members)] = ref[...]
        for i, ref in enumerate(refs[members : members + group]):
            fact_ref[lax.div(sender(member, i * tiles, members), tiles)] = ref[...]
        for j in range(min(group, max(0, WIN - group)), group):
            put_frame(
                out_ref, j, group, gain_ref, bias_ref, fact_ref, asked_ref, team_ref, before_ref, []
            )

    return pl.pallas_call(
        body,
        out_shape=[
            jax.ShapeDtypeStruct((members, tokens, width), jnp.bfloat16),
            jax.ShapeDtypeStruct(team.shape, jnp.bfloat16),
            jax.ShapeDtypeStruct((group,) + facts[0].shape, jnp.float32),
        ],
        in_specs=[SMEM] + [VMEM] * (3 + members + group),
        out_specs=[VMEM] * 3,
        cost_estimate=cost(group * width // HD * (WIN + 1), members // group * tokens),
        compiler_params=pltpu.CompilerParams(vmem_limit_bytes=48 * 1024 * 1024),
    )(gains, bias, asked, team, *ahead, *facts)


def attend_far(facts, asked, team, before, far, near, bias, gains, group):
    members, tokens, width = near.shape
    finished = min(group, max(0, WIN - group)) * members // group

    def body(gain_ref, bias_ref, fact_ref, asked_ref, team_ref, before_ref, near_ref, *refs):
        far_refs, outs, all_ref = refs[: len(far)], refs[len(far) : -1], refs[-1]
        if finished < members:
            all_ref[finished:] = near_ref[finished:]
        for j in range(finished * group // members):
            put_frame(
                all_ref,
                j,
                group,
                gain_ref,
                bias_ref,
                fact_ref,
                asked_ref,
                team_ref,
                before_ref,
                far_refs,
            )
        member = here(group, members // group)
        for m, out in enumerate(outs):
            out[...] = all_ref[partner(member, m, members)]

    return pl.pallas_call(
        body,
        out_shape=[jax.ShapeDtypeStruct((tokens, width), near.dtype)] * members,
        in_specs=[SMEM] + [VMEM] * (6 + len(far)),
        out_specs=[VMEM] * members,
        scratch_shapes=[pltpu.VMEM(near.shape, near.dtype)],
        cost_estimate=cost(width // HD * (WIN + 1), members // group * tokens),
        compiler_params=pltpu.CompilerParams(vmem_limit_bytes=48 * 1024 * 1024),
    )(gains, bias, facts, asked, team, before, near, *far)


def window_bias(mask_rows, tile_count):
    tile_cols = min(tile_count, 4)
    pos = jnp.arange(tile_count * TH * TW, dtype=jnp.int32)
    tile, within = pos // (TH * TW), pos % (TH * TW)
    row = (tile // tile_cols * TH + within // TW) // BLK
    col = (tile % tile_cols * TW + within % TW) // BLK
    down = row[None, :] - row[:, None]
    across = col[None, :] - col[:, None]
    near = (jnp.abs(down) <= 1) & (jnp.abs(across) <= 1)
    code = jnp.where(near, (down + 1) * 3 + across + 1, -1)
    allowed = (code == 4)[None]
    for offset in range(9):
        allowed = allowed | (code == offset)[None] & (mask_rows[:, offset] == 1)[:, None, None]
    return jnp.where(allowed, 0.0, NEG_BIG).astype(jnp.float32)


def shards(queries, keys, values, step_index, frame_index, window_mask, history_mask, step_gain):
    tile_count = lax.axis_size("tile")
    frame_count = lax.axis_size("frame")
    group = team_frames(frame_count, tile_count)
    members = group * tile_count
    teams = frame_count // group
    head_share = HEADS // members
    hops = -(-WIN // group)
    both = ("frame", "tile")

    def exchange(block):
        return lax.all_to_all(
            block,
            both,
            0,
            0,
            axis_index_groups=[[t * members + n for n in range(members)] for t in range(teams)],
            tiled=True,
        )

    def team_permute(block, ahead, m, around=True):
        route = [
            (t * members + n, (t + ahead) % teams * members + partner(n, m, members))
            for t in range(teams if around else teams - ahead)
            for n in range(members)
        ]
        return lax.ppermute(block, both, route)

    packed_kv, *ahead = pack_kv(keys[0, 0], values[0, 0], group, tile_count, head_share)
    sent = {}
    for m in [0, 2, 1, 3, 4, 6, 5, 7]:
        block = ahead[m]
        sent[m] = team_permute(block, 1, m)
    ahead = [sent[m] for m in range(members)]
    team = exchange(packed_kv)
    team, *some = lax.optimization_barrier((team, *[ahead[m] for m in [0, 2, 1, 3]]))
    for m, block in zip([0, 2, 1, 3], some):
        ahead[m] = block
    far, first = [], first_needed(2, group)
    for hop in range(2, hops + 1):
        needed = first_needed(hop, group)
        tail = team[needed * tile_count :, :, : 2 * STRAIGHT * HD]
        block = far[-1][(needed - first) * tile_count :] if far else pick_tail(ahead, group, tile_count)
        far += [team_permute(tail, hop, 0, False), team_permute(block, 1, 0, True)]
        first = needed
    asked, fact = pack_queries(history_mask, frame_index, step_index, queries[0, 0], members)
    asked, *some = lax.optimization_barrier((asked, *[ahead[m] for m in [1]]))
    for m, block in zip([1], some):
        ahead[m] = block
    asked = exchange(asked)
    fact, ahead[6] = lax.optimization_barrier((fact, ahead[6]))
    facts = [fact] + [team_permute(fact, 0, i * tile_count) for i in range(1, group)]

    share = here(group, tile_count) * head_share
    gains = lax.dynamic_slice(step_gain, (0, share), (STEPS, head_share))
    my_mask = lax.dynamic_slice(window_mask, (share, 0), (head_share, 9))
    bias = window_bias(my_mask, tile_count)
    team, far[0] = lax.optimization_barrier((team, far[0]))
    near, before, facts = attend_near(facts, asked, team, ahead, bias, gains, group)
    out = attend_far(facts, asked, team, before, far, near, bias, gains, group)
    order = [5, 4, 7, 6, 1, 3, 2, 0]
    back = {m: team_permute(out[m], 0, m) if m else out[m] for m in order}
    return unpack(back, group, tile_count, order)[None, None]


def solution(mesh):
    return jax.shard_map(
        shards,
        mesh=mesh,
        in_specs=(
            P("frame", "tile", None, None),
            P("frame", "tile", None, None),
            P("frame", "tile", None, None),
            P("frame"),
            P("frame"),
            P(),
            P("frame", None),
            P(),
        ),
        out_specs=P("frame", "tile", None, None),
        check_vma=False,
    )
```

```python
import functools
import math

import jax
import jax.numpy as jnp
from jax import lax
from jax.experimental import pallas as pl
from jax.experimental.pallas import tpu as pltpu
from jax.sharding import PartitionSpec as P

HEADS = 40
HD = 128
TH = 8
TW = 8
BLK = 4
WIN = 5
STEPS = 4

NEG_BIG = -1e30
FACT_ROWS = 8
STRAIGHT = 3

VMEM = pl.BlockSpec(memory_space=pltpu.VMEM)
SMEM = pl.BlockSpec(memory_space=pltpu.SMEM)


def team_frames(frame_count, tile_count):
    return max(
        g
        for g in range(1, frame_count + 1)
        if frame_count % g == 0 and HEADS % (g * tile_count) == 0
    )


def first_needed(hop, group):
    return max(0, hop * group - WIN)


def partner(member, m, members):
    return member ^ m if members & (members - 1) == 0 else (member + m) % members


def sender(member, m, members):
    return member ^ m if members & (members - 1) == 0 else (member - m) % members


def here(group, tiles):
    return lax.rem(lax.axis_index("frame"), group) * tiles + lax.axis_index("tile")


def pack_kv(own_k, own_v, group, tiles, head_share):
    tokens = own_k.shape[0]
    width = head_share * HD
    members = group * tiles

    def body(k_ref, v_ref, own, *outs):
        cut = STRAIGHT * HD
        for n in range(members):
            first, last = n * width, (n + 1) * width
            own[n, :, :cut] = k_ref[:, first : first + cut]
            own[n, :, cut : 2 * cut] = v_ref[:, first : first + cut]
            own[n, :, 2 * cut : width + cut] = k_ref[:, first + cut : last]
            own[n, :, width + cut :] = v_ref[:, first + cut : last]
        member = here(group, tiles)
        for m, out in enumerate(outs):
            out[...] = own[partner(member, m, members)]

    shape = (tokens, 2 * width)
    return pl.pallas_call(
        body,
        out_shape=[jax.ShapeDtypeStruct((members,) + shape, jnp.bfloat16)]
        + [jax.ShapeDtypeStruct(shape, jnp.bfloat16)] * members,
        in_specs=[VMEM] * 2,
        out_specs=[VMEM] * (1 + members),
    )(own_k, own_v)


def pick_tail(blocks, group, tiles):
    members = len(blocks)
    needed = first_needed(2, group) * tiles
    cut = 2 * STRAIGHT * HD

    def body(*refs):
        member = here(group, tiles)
        for m, ref in enumerate(refs[:-1]):
            place = sender(member, m, members) - needed

            @pl.when(place >= 0)
            def _():
                refs[-1][place] = ref[:, cut:]

    tokens, width = blocks[0].shape
    return pl.pallas_call(
        body,
        out_shape=jax.ShapeDtypeStruct((members - needed, tokens, width - cut), jnp.bfloat16),
        in_specs=[VMEM] * members,
        out_specs=VMEM,
        compiler_params=pltpu.CompilerParams(vmem_limit_bytes=16 * 1024 * 1024),
    )(*blocks)


def pack_queries(history, frame_index, step_index, own_q, members):
    tokens, channels = own_q.shape
    width = channels // members

    def body(history_ref, index_ref, step_ref, q_ref, out, fact_ref):
        row = lax.broadcasted_iota(jnp.int32, fact_ref.shape, 0)
        block = jnp.where(row == WIN, step_ref[0], 0)
        for d in range(1, WIN + 1):
            usable = (
                (history_ref[0, d - 1] == 1)
                & (d <= index_ref[0])
                & (d <= lax.axis_index("frame"))
            )
            block = jnp.where(row == d - 1, usable.astype(jnp.int32), block)
        fact_ref[...] = block.astype(jnp.float32)
        for n in range(members):
            out[n] = q_ref[:, n * width : (n + 1) * width]

    return pl.pallas_call(
        body,
        out_shape=[
            jax.ShapeDtypeStruct((members, tokens, width), jnp.bfloat16),
            jax.ShapeDtypeStruct((FACT_ROWS, HD), jnp.float32),
        ],
        in_specs=[SMEM] * 3 + [VMEM],
        out_specs=[VMEM] * 2,
    )(history, frame_index, step_index, own_q)


def unpack(blocks, group, tiles, order):
    members = len(blocks)
    tokens, width = blocks[0].shape

    def body(*refs):
        member = here(group, tiles)
        for m, ref in zip(order, refs[:-1]):
            lanes = pl.multiple_of(sender(member, m, members) * width, HD)
            refs[-1][:, pl.ds(lanes, width)] = ref[...]

    return pl.pallas_call(
        body,
        out_shape=jax.ShapeDtypeStruct((tokens, members * width), jnp.bfloat16),
        in_specs=[VMEM] * members,
        out_specs=VMEM,
        compiler_params=pltpu.CompilerParams(vmem_limit_bytes=16 * 1024 * 1024),
    )(*[blocks[m] for m in order])


FACTOR = math.log2(math.e) / math.sqrt(HD)


def frame_facts(facts, frame_tok):
    past = (facts - 1.0) * -NEG_BIG
    past = [past[d : d + 1] for d in range(WIN) for _ in range(frame_tok // HD)]
    return jnp.concatenate(past, axis=1), facts[WIN : WIN + 1]


def head_gain(gain_ref, step, h):
    gain = jnp.zeros((1, HD), jnp.float32)
    for s in range(STEPS):
        gain = jnp.where(step == s, gain_ref[s, h], gain)
    return gain


def kv_lanes(h, heads, straight=STRAIGHT):
    if h < straight:
        return h * HD, (straight + h) * HD
    return (straight + h) * HD, (heads + h) * HD


def rows_of(ref, row, tiles, lane):
    return ref[row : row + tiles, :, lane : lane + HD].reshape(-1, HD)


def scores_of(q, k):
    return FACTOR * lax.dot_general(
        q, k, (((1,), (1,)), ((), ())), preferred_element_type=jnp.float32
    )


def weigh(weights, v):
    v = jnp.concatenate([v, jnp.ones(v.shape, v.dtype)], axis=1)
    both = jnp.dot(weights.astype(jnp.bfloat16), v, preferred_element_type=jnp.float32)
    return both[:, :HD], both[:, HD:]


def cost(pairs, frame_tok):
    return pl.CostEstimate(
        flops=4 * pairs * frame_tok * frame_tok * HD,
        bytes_accessed=4 * pairs * frame_tok * HD,
        transcendentals=pairs * frame_tok * frame_tok,
    )


def put_frame(
    out_ref, j, group, gain_ref, bias_ref, fact_ref, asked_ref, team_ref, before_ref, far_refs
):
    members, tokens, width = out_ref.shape
    tiles = members // group
    frame_tok = tiles * tokens
    past, step = frame_facts(fact_ref[j], frame_tok)
    frames = []
    for d in range(WIN + 1):
        hop = max(0, -((j - d) // group))
        skipped = first_needed(hop, group) if hop > 1 else 0
        frames.append((hop, (j - d + hop * group - skipped) * tiles))
    for h in range(width // HD):
        lane = h * HD
        q = rows_of(asked_ref, j * tiles, tiles, lane)
        straight = h < STRAIGHT
        refs = [team_ref, before_ref, *far_refs[int(not straight) :: 2]]
        shift = 0 if straight else 2 * STRAIGHT * HD
        k, v = (
            jnp.concatenate(
                [rows_of(refs[hop], row, tiles, at - shift * (hop > 1)) for hop, row in frames]
            )
            for at in kv_lanes(h, width // HD)
        )
        scores = scores_of(q, k)
        scores = jnp.concatenate(
            [scores[:, :frame_tok] + bias_ref[h], scores[:, frame_tok:] + past], axis=1
        )
        weights = jnp.exp2(scores - jnp.max(scores, axis=1, keepdims=True))
        blended, norm = weigh(weights, v)
        result = (blended / norm * head_gain(gain_ref, step, h)).astype(jnp.bfloat16)
        out_ref[j * tiles : (j + 1) * tiles, :, lane : lane + HD] = result.reshape(
            tiles, tokens, HD
        )


def attend_near(facts, asked, team, ahead, bias, gains, group):
    members, tokens = team.shape[:2]
    width = team.shape[-1] // 2

    tiles = members // group

    def body(gain_ref, bias_ref, asked_ref, team_ref, *refs):
        out_ref, before_ref, fact_ref = refs[members + group :]
        member = here(group, tiles)
        for m, ref in enumerate(refs[:members]):
            before_ref[sender(member, m, members)] = ref[...]
        for i, ref in enumerate(refs[members : members + group]):
            fact_ref[lax.div(sender(member, i * tiles, members), tiles)] = ref[...]
        for j in range(min(group, max(0, WIN - group)), group):
            put_frame(
                out_ref, j, group, gain_ref, bias_ref, fact_ref, asked_ref, team_ref, before_ref, []
            )

    return pl.pallas_call(
        body,
        out_shape=[
            jax.ShapeDtypeStruct((members, tokens, width), jnp.bfloat16),
            jax.ShapeDtypeStruct(team.shape, jnp.bfloat16),
            jax.ShapeDtypeStruct((group,) + facts[0].shape, jnp.float32),
        ],
        in_specs=[SMEM] + [VMEM] * (3 + members + group),
        out_specs=[VMEM] * 3,
        cost_estimate=cost(group * width // HD * (WIN + 1), members // group * tokens),
        compiler_params=pltpu.CompilerParams(vmem_limit_bytes=48 * 1024 * 1024),
    )(gains, bias, asked, team, *ahead, *facts)


def attend_far(facts, asked, team, before, far, near, bias, gains, group):
    members, tokens, width = near.shape
    finished = min(group, max(0, WIN - group)) * members // group

    def body(gain_ref, bias_ref, fact_ref, asked_ref, team_ref, before_ref, near_ref, *refs):
        far_refs, outs, all_ref = refs[: len(far)], refs[len(far) : -1], refs[-1]
        if finished < members:
            all_ref[finished:] = near_ref[finished:]
        for j in range(finished * group // members):
            put_frame(
                all_ref,
                j,
                group,
                gain_ref,
                bias_ref,
                fact_ref,
                asked_ref,
                team_ref,
                before_ref,
                far_refs,
            )
        member = here(group, members // group)
        for m, out in enumerate(outs):
            out[...] = all_ref[partner(member, m, members)]

    return pl.pallas_call(
        body,
        out_shape=[jax.ShapeDtypeStruct((tokens, width), near.dtype)] * members,
        in_specs=[SMEM] + [VMEM] * (6 + len(far)),
        out_specs=[VMEM] * members,
        scratch_shapes=[pltpu.VMEM(near.shape, near.dtype)],
        cost_estimate=cost(width // HD * (WIN + 1), members // group * tokens),
        compiler_params=pltpu.CompilerParams(vmem_limit_bytes=48 * 1024 * 1024),
    )(gains, bias, facts, asked, team, before, near, *far)


def window_bias(mask_rows, tile_count):
    tile_cols = min(tile_count, 4)
    pos = jnp.arange(tile_count * TH * TW, dtype=jnp.int32)
    tile, within = pos // (TH * TW), pos % (TH * TW)
    row = (tile // tile_cols * TH + within // TW) // BLK
    col = (tile % tile_cols * TW + within % TW) // BLK
    down = row[None, :] - row[:, None]
    across = col[None, :] - col[:, None]
    near = (jnp.abs(down) <= 1) & (jnp.abs(across) <= 1)
    code = jnp.where(near, (down + 1) * 3 + across + 1, -1)
    allowed = (code == 4)[None]
    for offset in range(9):
        allowed = allowed | (code == offset)[None] & (mask_rows[:, offset] == 1)[:, None, None]
    return jnp.where(allowed, 0.0, NEG_BIG).astype(jnp.float32)


def shards(queries, keys, values, step_index, frame_index, window_mask, history_mask, step_gain):
    tile_count = lax.axis_size("tile")
    frame_count = lax.axis_size("frame")
    group = team_frames(frame_count, tile_count)
    members = group * tile_count
    teams = frame_count // group
    head_share = HEADS // members
    hops = -(-WIN // group)
    both = ("frame", "tile")

    def exchange(block):
        return lax.all_to_all(
            block,
            both,
            0,
            0,
            axis_index_groups=[[t * members + n for n in range(members)] for t in range(teams)],
            tiled=True,
        )

    def team_permute(block, ahead, m):
        route = [
            (t * members + n, (t + ahead) % teams * members + partner(n, m, members))
            for t in range(teams - ahead)
            for n in range(members)
        ]
        return lax.ppermute(block, both, route)

    packed_kv, *ahead = pack_kv(keys[0, 0], values[0, 0], group, tile_count, head_share)
    sent = {}
    for m in [0, 2, 1, 3, 4, 6, 5, 7]:
        block = ahead[m]
        sent[m] = team_permute(block, 1, m)
    ahead = [sent[m] for m in range(members)]
    team = exchange(packed_kv)
    team, *some = lax.optimization_barrier((team, *[ahead[m] for m in [0, 2, 1, 3]]))
    for m, block in zip([0, 2, 1, 3], some):
        ahead[m] = block
    far, first = [], first_needed(2, group)
    for hop in range(2, hops + 1):
        needed = first_needed(hop, group)
        tail = team[needed * tile_count :, :, : 2 * STRAIGHT * HD]
        block = far[-1][(needed - first) * tile_count :] if far else pick_tail(ahead, group, tile_count)
        far += [team_permute(tail, hop, 0), team_permute(block, 1, 0)]
        first = needed
    asked, fact = pack_queries(history_mask, frame_index, step_index, queries[0, 0], members)
    asked, *some = lax.optimization_barrier((asked, *[ahead[m] for m in [1]]))
    for m, block in zip([1], some):
        ahead[m] = block
    asked = exchange(asked)
    fact, ahead[6] = lax.optimization_barrier((fact, ahead[6]))
    facts = [fact] + [team_permute(fact, 0, i * tile_count) for i in range(1, group)]

    share = here(group, tile_count) * head_share
    gains = lax.dynamic_slice(step_gain, (0, share), (STEPS, head_share))
    my_mask = lax.dynamic_slice(window_mask, (share, 0), (head_share, 9))
    bias = window_bias(my_mask, tile_count)
    team, far[0] = lax.optimization_barrier((team, far[0]))
    near, before, facts = attend_near(facts, asked, team, ahead, bias, gains, group)
    out = attend_far(facts, asked, team, before, far, near, bias, gains, group)
    order = [5, 4, 7, 6, 1, 3, 2, 0]
    back = {m: team_permute(out[m], 0, m) if m else out[m] for m in order}
    return unpack(back, group, tile_count, order)[None, None]


def solution(mesh):
    return jax.shard_map(
        shards,
        mesh=mesh,
        in_specs=(
            P("frame", "tile", None, None),
            P("frame", "tile", None, None),
            P("frame", "tile", None, None),
            P("frame"),
            P("frame"),
            P(),
            P("frame", None),
            P(),
        ),
        out_specs=P("frame", "tile", None, None),
        check_vma=False,
    )
```
